32 devices in a mesh: cells: 8 (over z, x), slab: 4 (over y, core).
Axes of the slice: x: 2, y: 2, z: 4, core: 2. Of those that a mesh axis runs over, the one named last changes fastest.
Arguments:
- held_modes: bfloat16 [8192, 1024], P(('cells', 'slab')), may hold values from -5 to 5
- snapshots: bfloat16 [8192, 512], P(('cells', 'slab')), may hold values from -203 to 203
Outputs:
- basis_panel: float32 [8192, 512], P(('cells', 'slab'))
- factor_r: float32 [512, 512], replicated
The draws below stay inside these ranges and needn't reach their ends.
All inputs are finite; a program needn't handle non-finite values.
Results may differ from the reference program's by a relative error of at most 0.0006.
Values sent between devices are 32-bit elements; how exact they have to be, the bound alone decides.
A program may use at most 64 MiB of HBM per device.

```python
import math
import jax
import jax.numpy as jnp
from jax import lax

K = 1024
P_SIZE = 512
ROWS_DEV = 256
ROWS = 8192


def shared_modes(key):
    return jax.random.truncated_normal(key, -5.0, 5.0, (ROWS, K), jnp.float32)


def draw_held_modes(key, part):
    return shared_modes(key).astype(jnp.bfloat16)


def draw_snapshots(key, part):
    modes_full = shared_modes(key)
    key = jax.random.fold_in(key, 7)
    keys = jax.random.split(key, 5)
    leading = jax.random.uniform(keys[0], (1, P_SIZE), jnp.float32, 1.0, 3.0)
    second = jax.random.uniform(keys[1], (1, P_SIZE), jnp.float32, -1.5, 1.5)
    position = jnp.arange(ROWS, dtype=jnp.float32) / ROWS
    row_scale = jnp.exp(jax.random.uniform(keys[2], (ROWS, 1), jnp.float32, math.log(0.5), math.log(5.0)))
    row_scale = row_scale * (1.0 + 2.0 * position)[:, None]
    column_scale = jnp.exp(jax.random.uniform(keys[3], (1, P_SIZE), jnp.float32, math.log(0.3), math.log(3.0)))
    noise = jax.random.truncated_normal(keys[4], -4.0, 4.0, (ROWS, P_SIZE), jnp.float32)
    values = modes_full[:, :P_SIZE] * leading + modes_full[:, P_SIZE:2 * P_SIZE] * second + row_scale * column_scale * noise
    return values.astype(jnp.bfloat16)


def setup_inputs(seed: int = 0) -> dict:
    seeds = jax.random.split(jax.random.key(seed), 3)
    return {
        "held_modes": draw_held_modes(jax.random.fold_in(seeds[2], 71), 0),
        "snapshots": draw_snapshots(jax.random.fold_in(seeds[2], 71), 0),
    }


def reference(held_modes, snapshots):
    blocks = ROWS // ROWS_DEV
    mode_blocks = held_modes.reshape(blocks, ROWS_DEV, K)
    snap_blocks = snapshots.reshape(blocks, ROWS_DEV, P_SIZE)

    def project(running, pair):
        mode_block, snap_block = pair
        term = lax.dot_general(mode_block.astype(jnp.float32), snap_block.astype(jnp.float32), (((0,), (0,)), ((), ())), preferred_element_type=jnp.float32)
        return (running + term, None)
    summed, _ = lax.scan(project, jnp.zeros((K, P_SIZE), jnp.float32), (mode_blocks, snap_blocks))
    coefficients = summed / ROWS

    def residual_of(mode_block, snap_block):
        return snap_block.astype(jnp.float32) - jnp.dot(mode_block.astype(jnp.float32), coefficients, precision=lax.Precision.HIGHEST)

    def accumulate(running, pair):
        residual_block = residual_of(pair[0], pair[1])
        term = lax.dot_general(residual_block, residual_block, (((0,), (0,)), ((), ())), precision=lax.Precision.HIGHEST)
        return (running + term, None)
    gram_sum, _ = lax.scan(accumulate, jnp.zeros((P_SIZE, P_SIZE), jnp.float32), (mode_blocks, snap_blocks))
    gram = gram_sum / ROWS
    lower_factor = jnp.linalg.cholesky(gram)

    def solve_block(pair):
        residual_block = residual_of(pair[0], pair[1])
        return lax.linalg.triangular_solve(lower_factor, residual_block, left_side=False, lower=True, transpose_a=True)
    basis_panel = lax.map(solve_block, (mode_blocks, snap_blocks)).reshape(ROWS, P_SIZE)
    return (basis_panel, lower_factor.T)
```

```python
import functools

import jax
import jax.numpy as jnp
from jax import lax
from jax.experimental import pallas as pl
from jax.experimental.pallas import tpu as pltpu
from jax.sharding import PartitionSpec as P

BLOCK = 128
HIGHEST = lax.Precision.HIGHEST


def dot(first, second, dims):
    return lax.dot_general(
        first, second, ((dims[:1], dims[1:]), ((), ())), precision=HIGHEST, preferred_element_type=jnp.float32
    )


def factor_block(rows):
    groups = len(rows)
    lane = lax.broadcasted_iota(jnp.int32, (8, BLOCK), 1)
    sub = lax.broadcasted_iota(jnp.int32, (8, BLOCK), 0)
    rows = list(rows)
    upper, inverse = [], []

    def lanes(value, index):
        return jnp.broadcast_to(value[:, index : index + 1], (8, BLOCK))

    def subs(value, index):
        return jnp.broadcast_to(value[index : index + 1, :], (8, BLOCK))

    for group in range(groups):
        first = 8 * group
        panel = rows[group]
        columns = [lanes(panel, first + k) for k in range(8)]
        outer = [[lanes(rows[other], first + k) for k in range(8)] for other in range(group + 1, groups)]
        scaled = jnp.zeros((8, BLOCK), jnp.float32)
        diagonal = jnp.zeros((8, BLOCK), jnp.float32)
        for j in range(8):
            here = sub == j
            column = columns[j]
            root = lax.rsqrt(subs(column, j))
            scaled_row = subs(panel, j) * root
            scaled = jnp.where(here, scaled_row, scaled)
            diagonal = jnp.where(here, root, diagonal)
            pivot_row = jnp.where(lane == first + j, root, scaled_row) * root
            weight = jnp.where(here, -1.0, column)
            panel = jnp.where(here | (lane == first + j), 0.0, panel) - weight * pivot_row
            for k in range(j + 1, 8):
                entry = subs(columns[k], j) * (root * root)
                columns[k] = jnp.where(here, 0.0, columns[k]) - weight * entry
        row_index = sub + first
        upper.append(jnp.where(lane >= row_index, scaled, 0.0))
        inverse.append(jnp.where(lane < row_index, scaled, jnp.where(lane == row_index, diagonal, 0.0)))
        solved = [subs(panel, k) for k in range(8)]
        kept = (lane < first) | (lane >= first + 8)
        for other in range(group + 1, groups):
            terms = [outer[other - group - 1][k] * solved[k] for k in range(8)]
            while len(terms) > 1:
                terms = [a + b for a, b in zip(terms[::2], terms[1::2])]
            rows[other] = jnp.where(kept, rows[other], 0.0) - terms[0]
    return jnp.concatenate(upper, 0), jnp.concatenate(inverse, 0)


def factor_kernel(gram_ref, panel_ref, basis_ref, factor_ref, schur, residual):
    size = gram_ref.shape[0]
    schur[...] = gram_ref[...]
    residual[...] = panel_ref[...]
    column = lax.broadcasted_iota(jnp.int32, (BLOCK, size), 1)

    def step(block, carry):
        start = pl.multiple_of(block * BLOCK, BLOCK)
        here = pl.ds(start, BLOCK)
        rows = [schur[pl.ds(pl.multiple_of(start + 8 * g, 8), 8), here] for g in range(BLOCK // 8)]
        upper, inverse = factor_block(rows)
        beyond = dot(inverse, schur[here, :], (1, 0))
        beyond = jnp.where(column >= start + BLOCK, beyond, 0.0)
        schur[...] -= dot(beyond, beyond, (0, 0))
        factor_ref[here, :] = beyond
        factor_ref[here, here] = upper
        part = dot(residual[:, here], inverse, (1, 1))
        basis_ref[:, here] = part
        residual[...] -= dot(part, beyond, (1, 0))
        return carry

    lax.fori_loop(0, size // BLOCK, step, 0)


def factor(gram, residual_panel):
    rows, size = residual_panel.shape
    return pl.pallas_call(
        factor_kernel,
        out_shape=(
            jax.ShapeDtypeStruct((rows, size), jnp.float32),
            jax.ShapeDtypeStruct((size, size), jnp.float32),
        ),
        in_specs=[pl.BlockSpec(memory_space=pltpu.VMEM)] * 2,
        out_specs=(pl.BlockSpec(memory_space=pltpu.VMEM),) * 2,
        scratch_shapes=[pltpu.VMEM((size, size), jnp.float32), pltpu.VMEM((rows, size), jnp.float32)],
        compiler_params=pltpu.CompilerParams(vmem_limit_bytes=32 * 1024 * 1024),
        name="factor",
    )(gram, residual_panel)


def local(held_modes, snapshots):
    total_rows = held_modes.shape[0] * lax.axis_size("cells") * lax.axis_size("slab")
    local_terms = lax.dot_general(
        held_modes, snapshots, (((0,), (0,)), ((), ())), preferred_element_type=jnp.float32
    )
    summed = lax.psum(local_terms, ("cells", "slab"))
    coefficients = summed / total_rows
    residual_panel = snapshots.astype(jnp.float32) - jnp.dot(
        held_modes.astype(jnp.float32), coefficients, precision=HIGHEST
    )
    gram = lax.psum(dot(residual_panel, residual_panel, (0, 0)), ("cells", "slab")) / total_rows
    return factor(gram, residual_panel)


def solution(mesh):
    in_specs = (P(("cells", "slab"), None), P(("cells", "slab"), None))
    out_specs = (P(("cells", "slab"), None), P())
    return jax.shard_map(local, mesh=mesh, in_specs=in_specs, out_specs=out_specs, check_vma=False)
```

```python
import functools

import jax
import jax.numpy as jnp
from jax import lax
from jax.experimental import pallas as pl
from jax.experimental.pallas import tpu as pltpu
from jax.sharding import PartitionSpec as P

BLOCK = 128
MESH = pl.DeviceIdType.MESH
HIGHEST = lax.Precision.HIGHEST


def dot(first, second, dims):
    return lax.dot_general(
        first, second, ((dims[:1], dims[1:]), ((), ())), precision=HIGHEST, preferred_element_type=jnp.float32
    )


def factor_block(rows):
    groups = len(rows)
    lane = lax.broadcasted_iota(jnp.int32, (8, BLOCK), 1)
    sub = lax.broadcasted_iota(jnp.int32, (8, BLOCK), 0)
    rows = list(rows)
    upper, inverse = [], []

    def lanes(value, index):
        return jnp.broadcast_to(value[:, index : index + 1], (8, BLOCK))

    def subs(value, index):
        return jnp.broadcast_to(value[index : index + 1, :], (8, BLOCK))

    for group in range(groups):
        first = 8 * group
        panel = rows[group]
        columns = [lanes(panel, first + k) for k in range(8)]
        outer = [[lanes(rows[other], first + k) for k in range(8)] for other in range(group + 1, groups)]
        scaled = jnp.zeros((8, BLOCK), jnp.float32)
        diagonal = jnp.zeros((8, BLOCK), jnp.float32)
        for j in range(8):
            here = sub == j
            column = columns[j]
            root = lax.rsqrt(subs(column, j))
            scaled_row = subs(panel, j) * root
            scaled = jnp.where(here, scaled_row, scaled)
            diagonal = jnp.where(here, root, diagonal)
            pivot_row = jnp.where(lane == first + j, root, scaled_row) * root
            weight = jnp.where(here, -1.0, column)
            panel = jnp.where(here | (lane == first + j), 0.0, panel) - weight * pivot_row
            for k in range(j + 1, 8):
                entry = subs(columns[k], j) * (root * root)
                columns[k] = jnp.where(here, 0.0, columns[k]) - weight * entry
        row_index = sub + first
        upper.append(jnp.where(lane >= row_index, scaled, 0.0))
        inverse.append(jnp.where(lane < row_index, scaled, jnp.where(lane == row_index, diagonal, 0.0)))
        solved = [subs(panel, k) for k in range(8)]
        kept = (lane < first) | (lane >= first + 8)
        for other in range(group + 1, groups):
            terms = [outer[other - group - 1][k] * solved[k] for k in range(8)]
            while len(terms) > 1:
                terms = [a + b for a, b in zip(terms[::2], terms[1::2])]
            rows[other] = jnp.where(kept, rows[other], 0.0) - terms[0]
    return jnp.concatenate(upper, 0), jnp.concatenate(inverse, 0)


def upper_blocks(size):
    count = size // BLOCK
    return [(i, j) for i in range(count) for j in range(i, count)]


class Part:
    def __init__(self, start, rows, stages, sems):
        self.start, self.rows, self.stages, self.sems = start, rows, stages, sems
        self.spans = [(start, rows)]
        for stage in stages:
            at, n = self.spans[-1]
            n //= stage["count"]
            self.spans.append((at + stage["index"] * n, n))


def slice_of(start, rows):
    return pl.ds(pl.multiple_of(start, 8), rows)


def all_reduce(acc, total, landing, places, produce, scale, send_sems, recv_sems, started):
    core, pair, plane, line = places
    half = acc.shape[0] // 2
    unit = 8 * plane["count"] * line["count"]
    long_rows = max(1, round(0.75 * (half // unit))) * unit
    used = [0]

    def copy(src, dst, device):
        index = used[0]
        used[0] += 1
        descriptor = pltpu.make_async_remote_copy(
            src_ref=src,
            dst_ref=dst,
            send_sem=send_sems.at[index],
            recv_sem=recv_sems.at[index],
            device_id=device,
            device_id_type=MESH,
        )
        descriptor.start()
        started.append(descriptor)
        return descriptor

    mine, other = core * half, (1 - core) * half
    bounds = [(0, long_rows, (plane, line))]
    if half > long_rows:
        bounds.append((long_rows, half - long_rows, (line, plane)))
    parts = [Part(mine + at, n, stages, None) for at, n, stages in bounds]
    slot = [0]

    def room(count, rows):
        at = slot[0]
        slot[0] += count * rows
        return [landing.at[pl.ds(at + k * rows, rows)] for k in range(count)]

    firsts = []
    for at, n, _ in bounds:
        produce(other + at, n)
        span = room(1, n)[0]
        firsts.append((copy(acc.at[slice_of(other + at, n)], span, pair), span))
    for at, n, _ in bounds:
        produce(mine + at, n)
    for part, (first, span) in zip(parts, firsts):
        first.wait_recv()
        where = slice_of(part.start, part.rows)
        acc[where, :] = acc[where, :] + span[...]

    def send_scatter(part, level):
        stage = part.stages[level]
        at, _ = part.spans[level]
        n = part.spans[level + 1][1]
        spans = room(stage["count"] - 1, n)
        part.pending = [
            (copy(acc.at[slice_of(at + target * n, n)], span, device), span)
            for (target, device, _), span in zip(stage["peers"], spans)
        ]

    def finish_scatter(part, level):
        where = slice_of(*part.spans[level + 1])
        value = acc[where, :]
        for descriptor, span in part.pending:
            descriptor.wait_recv()
            value = value + span[...]
        if level + 1 == len(part.stages):
            total[where, :] = value * scale
        else:
            acc[where, :] = value

    def send_gather(part, level):
        where = slice_of(*part.spans[level + 1])
        part.pending = [
            copy(total.at[where], total.at[where], device) for _, device, _ in part.stages[level]["peers"]
        ]

    lasts = []

    def forward(start, n):
        where = slice_of(start, n)
        lasts.append(copy(total.at[where], total.at[where], pair))

    for part in parts:
        send_scatter(part, 0)
    for part in parts[::-1]:
        finish_scatter(part, 0)
        send_scatter(part, 1)
    for part in parts[::-1]:
        finish_scatter(part, 1)
        send_gather(part, 1)
    for part in parts[::-1]:
        for descriptor in part.pending:
            descriptor.wait_recv()
        send_gather(part, 0)
        forward(*part.spans[1])
    for part in parts[::-1]:
        at, _ = part.spans[0]
        n = part.spans[1][1]
        for descriptor, (_, _, source) in zip(part.pending, part.stages[0]["peers"]):
            descriptor.wait_recv()
            forward(at + source * n, n)
    for descriptor in lasts:
        descriptor.wait_recv()


def panel_kernel(
    line_count, total_rows, modes_ref, snaps_ref, residual_ref, gram_ref,
    terms, coefficients, landing, gram_terms, gram, gram_landing, send_sems, recv_sems, gram_send_sems, gram_recv_sems,
):
    cells, slab = lax.axis_index("cells"), lax.axis_index("slab")
    z, x, y, core = cells // 2, cells % 2, slab // 2, slab % 2
    pair = {"cells": cells, "slab": y * 2 + (1 - core)}
    plane_peers = []
    for k in range(1, 4):
        there_x = 1 - x if k & 2 else x
        there_y = 1 - y if k & 1 else y
        device = {"cells": z * 2 + there_x, "slab": there_y * 2 + core}
        plane_peers.append((there_x * 2 + there_y, device, there_x * 2 + there_y))
    line_peers = []
    for k in range(1, line_count):
        ahead, behind = lax.rem(z + k, line_count), lax.rem(z + line_count - k, line_count)
        line_peers.append((ahead, {"cells": ahead * 2 + x, "slab": slab}, behind))
    plane = {"count": 4, "index": x * 2 + y, "peers": plane_peers}
    line = {"count": line_count, "index": z, "peers": line_peers}
    places = (core, pair, plane, line)

    devices = [pair] + [peer[1] for peer in plane_peers + line_peers]
    barrier = pltpu.get_barrier_semaphore()
    for device in devices:
        pl.semaphore_signal(barrier, inc=1, device_id=device, device_id_type=MESH)

    started = []
    scale = 1.0 / total_rows
    entered = []

    def project(start, rows):
        wanted = modes_ref[:, pl.ds(pl.multiple_of(start, BLOCK), rows)]
        terms[slice_of(start, rows), :] = lax.dot_general(
            wanted, snaps_ref[...], (((0,), (0,)), ((), ())), preferred_element_type=jnp.float32
        )
        if not entered:
            pl.semaphore_wait(barrier, len(devices))
            entered.append(True)

    all_reduce(terms, coefficients, landing, places, project, scale, send_sems, recv_sems, started)

    def times(part):
        return jnp.dot(modes_ref[...], part, preferred_element_type=jnp.float32)

    whole = coefficients[...]
    high = whole.astype(jnp.bfloat16)
    rest = whole - high.astype(jnp.float32)
    middle = rest.astype(jnp.bfloat16)
    low = (rest - middle.astype(jnp.float32)).astype(jnp.bfloat16)
    residual_ref[...] = snaps_ref[...].astype(jnp.float32) - (times(high) + (times(middle) + times(low)))

    size = residual_ref.shape[1]
    blocks = upper_blocks(size)
    for i in range(size // BLOCK):
        row = dot(residual_ref[:, i * BLOCK : (i + 1) * BLOCK], residual_ref[:, i * BLOCK :], (0, 0))
        for j in range(i, size // BLOCK):
            at = blocks.index((i, j)) * BLOCK
            gram_terms[at : at + BLOCK, :] = row[:, (j - i) * BLOCK : (j - i + 1) * BLOCK]
    all_reduce(
        gram_terms, gram, gram_landing, places, lambda start, rows: None, scale, gram_send_sems, gram_recv_sems, started
    )
    gram_ref[...] = gram[...]
    for descriptor in started:
        descriptor.wait_send()


def panel(held_modes, snapshots, line_count, total_rows):
    rows, modes = held_modes.shape
    size = snapshots.shape[1]
    gram_rows = len(upper_blocks(size)) * BLOCK
    count = 2 * (1 + 2 * (3 + line_count - 1) + max(4, line_count))
    sems = pltpu.SemaphoreType.DMA((count,))
    return pl.pallas_call(
        functools.partial(panel_kernel, line_count, total_rows),
        out_shape=(
            jax.ShapeDtypeStruct((rows, size), jnp.float32),
            jax.ShapeDtypeStruct((gram_rows, BLOCK), jnp.float32),
        ),
        in_specs=[pl.BlockSpec(memory_space=pltpu.VMEM)] * 2,
        out_specs=(pl.BlockSpec(memory_space=pltpu.VMEM),) * 2,
        scratch_shapes=[
            pltpu.VMEM((modes, size), jnp.float32),
            pltpu.VMEM((modes, size), jnp.float32),
            pltpu.VMEM((2 * modes, size), jnp.float32),
            pltpu.VMEM((gram_rows, BLOCK), jnp.float32),
            pltpu.VMEM((gram_rows, BLOCK), jnp.float32),
            pltpu.VMEM((2 * gram_rows, BLOCK), jnp.float32),
            sems, sems, sems, sems,
        ],
        compiler_params=pltpu.CompilerParams(
            collective_id=0, has_side_effects=True, vmem_limit_bytes=40 * 1024 * 1024
        ),
        name="panel",
    )(held_modes, snapshots)


def factor_kernel(gram_ref, panel_ref, basis_ref, factor_ref, schur, residual):
    size = schur.shape[0]
    schur[...] = jnp.zeros_like(schur)
    for index, (i, j) in enumerate(upper_blocks(size)):
        block = gram_ref[index * BLOCK : (index + 1) * BLOCK, :]
        schur[i * BLOCK : (i + 1) * BLOCK, j * BLOCK : (j + 1) * BLOCK] = block
    residual[...] = panel_ref[...]
    column = lax.broadcasted_iota(jnp.int32, (BLOCK, size), 1)

    def step(block, carry):
        start = pl.multiple_of(block * BLOCK, BLOCK)
        here = pl.ds(start, BLOCK)
        rows = [schur[pl.ds(pl.multiple_of(start + 8 * g, 8), 8), here] for g in range(BLOCK // 8)]
        upper, inverse = factor_block(rows)
        beyond = dot(inverse, schur[here, :], (1, 0))
        beyond = jnp.where(column >= start + BLOCK, beyond, 0.0)
        schur[...] -= dot(beyond, beyond, (0, 0))
        factor_ref[here, :] = beyond
        factor_ref[here, here] = upper
        part = dot(residual[:, here], inverse, (1, 1))
        basis_ref[:, here] = part
        residual[...] -= dot(part, beyond, (1, 0))
        return carry

    lax.fori_loop(0, size // BLOCK, step, 0)


def factor(gram, residual_panel):
    rows, size = residual_panel.shape
    return pl.pallas_call(
        factor_kernel,
        out_shape=(
            jax.ShapeDtypeStruct((rows, size), jnp.float32),
            jax.ShapeDtypeStruct((size, size), jnp.float32),
        ),
        in_specs=[pl.BlockSpec(memory_space=pltpu.VMEM)] * 2,
        out_specs=(pl.BlockSpec(memory_space=pltpu.VMEM),) * 2,
        scratch_shapes=[pltpu.VMEM((size, size), jnp.float32), pltpu.VMEM((rows, size), jnp.float32)],
        compiler_params=pltpu.CompilerParams(vmem_limit_bytes=32 * 1024 * 1024),
        name="factor",
    )(gram, residual_panel)


def local(held_modes, snapshots):
    cells, slab = lax.axis_size("cells"), lax.axis_size("slab")
    total_rows = held_modes.shape[0] * cells * slab
    size = snapshots.shape[1]
    blocks = upper_blocks(size)
    line_count = cells // 2
    unit = 8 * 4 * line_count
    halves = (held_modes.shape[1] // 2, len(blocks) * BLOCK // 2)
    if slab == 4 and cells % 2 == 0 and all(half % unit == 0 for half in halves):
        return factor(*panel(held_modes, snapshots, line_count, total_rows)[::-1])
    local_terms = lax.dot_general(
        held_modes, snapshots, (((0,), (0,)), ((), ())), preferred_element_type=jnp.float32
    )
    coefficients = lax.psum(local_terms, ("cells", "slab")) / total_rows
    residual_panel = snapshots.astype(jnp.float32) - jnp.dot(
        held_modes.astype(jnp.float32), coefficients, precision=HIGHEST
    )
    gram = lax.psum(dot(residual_panel, residual_panel, (0, 0)), ("cells", "slab")) / total_rows
    packed = [gram[i * BLOCK : (i + 1) * BLOCK, j * BLOCK : (j + 1) * BLOCK] for i, j in blocks]
    return factor(jnp.concatenate(packed, 0), residual_panel)


def solution(mesh):
    in_specs = (P(("cells", "slab"), None), P(("cells", "slab"), None))
    out_specs = (P(("cells", "slab"), None), P())
    return jax.shard_map(local, mesh=mesh, in_specs=in_specs, out_specs=out_specs, check_vma=False)
```

```python
import functools

import jax
import jax.numpy as jnp
from jax import lax
from jax.experimental import pallas as pl
from jax.experimental.pallas import tpu as pltpu
from jax.sharding import PartitionSpec as P

BLOCK = 128
MESH = pl.DeviceIdType.MESH
CHUNKS = 2
STEPS = 7
HIGHEST = lax.Precision.HIGHEST


def dot(first, second, dims):
    return lax.dot_general(
        first, second, ((dims[:1], dims[1:]), ((), ())), precision=HIGHEST, preferred_element_type=jnp.float32
    )


def factor_block(rows):
    groups = len(rows)
    lane = lax.broadcasted_iota(jnp.int32, (8, BLOCK), 1)
    sub = lax.broadcasted_iota(jnp.int32, (8, BLOCK), 0)
    rows = list(rows)
    upper, inverse = [], []

    def lanes(value, index):
        return jnp.broadcast_to(value[:, index : index + 1], (8, BLOCK))

    def subs(value, index):
        return jnp.broadcast_to(value[index : index + 1, :], (8, BLOCK))

    for group in range(groups):
        first = 8 * group
        panel = rows[group]
        columns = [lanes(panel, first + k) for k in range(8)]
        outer = [[lanes(rows[other], first + k) for k in range(8)] for other in range(group + 1, groups)]
        scaled = jnp.zeros((8, BLOCK), jnp.float32)
        diagonal = jnp.zeros((8, BLOCK), jnp.float32)
        for j in range(8):
            here = sub == j
            column = columns[j]
            root = lax.rsqrt(subs(column, j))
            scaled_row = subs(panel, j) * root
            scaled = jnp.where(here, scaled_row, scaled)
            diagonal = jnp.where(here, root, diagonal)
            pivot_row = jnp.where(lane == first + j, root, scaled_row) * root
            weight = jnp.where(here, -1.0, column)
            panel = jnp.where(here | (lane == first + j), 0.0, panel) - weight * pivot_row
            for k in range(j + 1, 8):
                entry = subs(columns[k], j) * (root * root)
                columns[k] = jnp.where(here, 0.0, columns[k]) - weight * entry
        row_index = sub + first
        upper.append(jnp.where(lane >= row_index, scaled, 0.0))
        inverse.append(jnp.where(lane < row_index, scaled, jnp.where(lane == row_index, diagonal, 0.0)))
        solved = [subs(panel, k) for k in range(8)]
        kept = (lane < first) | (lane >= first + 8)
        for other in range(group + 1, groups):
            terms = [outer[other - group - 1][k] * solved[k] for k in range(8)]
            while len(terms) > 1:
                terms = [a + b for a, b in zip(terms[::2], terms[1::2])]
            rows[other] = jnp.where(kept, rows[other], 0.0) - terms[0]
    return jnp.concatenate(upper, 0), jnp.concatenate(inverse, 0)


class Part:
    def __init__(self, start, rows, stages):
        self.start, self.rows, self.stages, self.pending = start, rows, stages, []
        self.spans = [(start, rows)]
        for stage in stages:
            at, n = self.spans[-1]
            n //= stage["count"]
            self.spans.append((at + stage["index"] * n, n))


def slice_of(start, rows):
    return pl.ds(pl.multiple_of(start, 8), rows)


def all_reduce(acc, total, landing, places, produce, scale, send_sems, recv_sems, started):
    core, pair, plane, line = places
    half = acc.shape[0] // 2
    unit = 8 * plane["count"] * line["count"]
    long_rows = max(1, round(0.75 * (half // unit))) * unit
    used = [0]

    def copy(src, dst, device):
        index = used[0]
        used[0] += 1
        descriptor = pltpu.make_async_remote_copy(
            src_ref=src,
            dst_ref=dst,
            send_sem=send_sems.at[index],
            recv_sem=recv_sems.at[index],
            device_id=device,
            device_id_type=MESH,
        )
        descriptor.start()
        started.append(descriptor)
        return descriptor

    mine, other = core * half, (1 - core) * half
    bounds = [(0, long_rows, (plane, line))]
    if half > long_rows:
        bounds.append((long_rows, half - long_rows, (line, plane)))
    parts = [Part(mine + at, n, stages) for at, n, stages in bounds]
    slot = [0]

    def room(count, rows):
        at = slot[0]
        slot[0] += count * rows
        return [landing.at[pl.ds(at + k * rows, rows)] for k in range(count)]

    def send_scatter(part, level):
        stage = part.stages[level]
        at, _ = part.spans[level]
        n = part.spans[level + 1][1]
        spans = room(stage["count"] - 1, n)
        part.pending = [
            (copy(acc.at[slice_of(at + target * n, n)], span, device), span)
            for (target, device, _), span in zip(stage["peers"], spans)
        ]

    def finish_scatter(part, level):
        where = slice_of(*part.spans[level + 1])
        value = acc[where, :]
        for descriptor, span in part.pending:
            descriptor.wait_recv()
            value = value + span[...]
        if level + 1 == len(part.stages):
            total[where, :] = value * scale
        else:
            acc[where, :] = value

    def send_gather(part, level):
        where = slice_of(*part.spans[level + 1])
        part.pending = [
            copy(total.at[where], total.at[where], device) for _, device, _ in part.stages[level]["peers"]
        ]

    lasts = []

    def forward(start, n):
        where = slice_of(start, n)
        lasts.append(copy(total.at[where], total.at[where], pair))

    firsts = []
    for at, n, _ in bounds:
        produce(other + at, n)
        span = room(1, n)[0]
        firsts.append((copy(acc.at[slice_of(other + at, n)], span, pair), span))
    for at, n, _ in bounds:
        produce(mine + at, n)
    yield
    for part, (first, span) in zip(parts, firsts):
        first.wait_recv()
        where = slice_of(part.start, part.rows)
        acc[where, :] = acc[where, :] + span[...]
        send_scatter(part, 0)
    yield
    for level in (0, 1):
        for part in parts[::-1]:
            finish_scatter(part, level)
            if level == 0:
                send_scatter(part, 1)
            else:
                send_gather(part, 1)
        yield
    for part in parts[::-1]:
        for descriptor in part.pending:
            descriptor.wait_recv()
        send_gather(part, 0)
        forward(*part.spans[1])
    yield
    for part in parts[::-1]:
        at, _ = part.spans[0]
        n = part.spans[1][1]
        for descriptor, (_, _, source) in zip(part.pending, part.stages[0]["peers"]):
            descriptor.wait_recv()
            forward(at + source * n, n)
    yield
    for descriptor in lasts:
        descriptor.wait_recv()


def panel_kernel(
    line_count, total_rows, modes_hbm, snaps_hbm, residual_ref, gram_ref, modes_ref, snaps_ref, load_sems,
    terms, coefficients, landing, gram_terms, gram, gram_landing, send_sems, recv_sems,
):
    loads = [
        pltpu.make_async_copy(modes_hbm, modes_ref, load_sems.at[0]),
        pltpu.make_async_copy(snaps_hbm, snaps_ref, load_sems.at[1]),
    ]
    for load in loads:
        load.start()
    cells, slab = lax.axis_index("cells"), lax.axis_index("slab")
    z, x, y, core = cells // 2, cells % 2, slab // 2, slab % 2
    pair = {"cells": cells, "slab": y * 2 + (1 - core)}
    plane_peers = []
    for k in range(1, 4):
        there_x = 1 - x if k & 2 else x
        there_y = 1 - y if k & 1 else y
        device = {"cells": z * 2 + there_x, "slab": there_y * 2 + core}
        plane_peers.append((there_x * 2 + there_y, device, there_x * 2 + there_y))
    line_peers = []
    for k in range(1, line_count):
        ahead, behind = lax.rem(z + k, line_count), lax.rem(z + line_count - k, line_count)
        line_peers.append((ahead, {"cells": ahead * 2 + x, "slab": slab}, behind))
    plane = {"count": 4, "index": x * 2 + y, "peers": plane_peers}
    line = {"count": line_count, "index": z, "peers": line_peers}
    places = (core, pair, plane, line)

    devices = [pair] + [peer[1] for peer in plane_peers + line_peers]
    barrier = pltpu.get_barrier_semaphore()
    for device in devices:
        pl.semaphore_signal(barrier, inc=1, device_id=device, device_id_type=MESH)

    for load in loads:
        load.wait()

    started = []
    scale = 1.0 / total_rows
    entered = []
    size = residual_ref.shape[1]
    width = size // CHUNKS

    def coefficient_sum(chunk):
        acc = terms.at[chunk]

        def project(start, rows):
            wanted = modes_ref[:, pl.ds(pl.multiple_of(start, BLOCK), rows)]
            acc[slice_of(start, rows), :] = lax.dot_general(
                wanted, snaps_ref[:, chunk * width : (chunk + 1) * width], (((0,), (0,)), ((), ())),
                preferred_element_type=jnp.float32,
            )
            if not entered:
                pl.semaphore_wait(barrier, len(devices))
                entered.append(True)

        return all_reduce(
            acc, coefficients.at[chunk], landing.at[chunk], places, project, scale,
            send_sems.at[chunk], recv_sems.at[chunk], started,
        )

    def gram_sum(chunk):
        rows = pl.ds(0, (chunk + 1) * width)
        return all_reduce(
            gram_terms.at[chunk, rows], gram.at[chunk, rows], gram_landing.at[chunk], places, lambda start, n: None,
            scale, send_sems.at[CHUNKS + chunk], recv_sems.at[CHUNKS + chunk], started,
        )

    def times(part):
        return jnp.dot(modes_ref[...], part, preferred_element_type=jnp.float32)

    def subtract(chunk):
        columns = slice(chunk * width, (chunk + 1) * width)
        whole = coefficients[chunk]
        high = whole.astype(jnp.bfloat16)
        rest = whole - high.astype(jnp.float32)
        middle = rest.astype(jnp.bfloat16)
        low = (rest - middle.astype(jnp.float32)).astype(jnp.bfloat16)
        value = snaps_ref[:, columns].astype(jnp.float32) - (times(high) + (times(middle) + times(low)))
        residual_ref[:, columns] = value
        before = (chunk + 1) * width
        gram_terms[chunk, :before, :] = dot(residual_ref[:, :before], value, (0, 0))

    sums = [coefficient_sum(chunk) for chunk in range(CHUNKS)]
    gram_sums = [gram_sum(chunk) for chunk in range(CHUNKS)]
    for _ in range(STEPS - 1):
        for turn in sums:
            next(turn)
    for chunk in range(CHUNKS):
        next(sums[chunk], None)
        subtract(chunk)
        next(gram_sums[chunk])
    for _ in range(STEPS - 1):
        for turn in gram_sums:
            next(turn, None)
    for chunk in range(CHUNKS):
        before, columns = (chunk + 1) * width, slice(chunk * width, (chunk + 1) * width)
        gram_ref[:before, columns] = gram[chunk, :before, :]
        if before < size:
            gram_ref[before:, columns] = jnp.zeros((size - before, width), jnp.float32)
    for descriptor in started:
        descriptor.wait_send()


def panel(held_modes, snapshots, line_count, total_rows):
    rows, modes = held_modes.shape
    size = snapshots.shape[1]
    width = size // CHUNKS
    count = 2 * (1 + 2 * (3 + line_count - 1) + max(4, line_count))
    return pl.pallas_call(
        functools.partial(panel_kernel, line_count, total_rows),
        out_shape=(
            jax.ShapeDtypeStruct((rows, size), jnp.float32),
            jax.ShapeDtypeStruct((size, size), jnp.float32),
        ),
        in_specs=[pl.BlockSpec(memory_space=pl.ANY)] * 2,
        out_specs=(pl.BlockSpec(memory_space=pltpu.VMEM),) * 2,
        scratch_shapes=[
            pltpu.VMEM((rows, modes), held_modes.dtype),
            pltpu.VMEM((rows, size), snapshots.dtype),
            pltpu.SemaphoreType.DMA((2,)),
            pltpu.VMEM((CHUNKS, modes, width), jnp.float32),
            pltpu.VMEM((CHUNKS, modes, width), jnp.float32),
            pltpu.VMEM((CHUNKS, 2 * modes, width), jnp.float32),
            pltpu.VMEM((CHUNKS, size, width), jnp.float32),
            pltpu.VMEM((CHUNKS, size, width), jnp.float32),
            pltpu.VMEM((CHUNKS, 2 * size, width), jnp.float32),
            pltpu.SemaphoreType.DMA((2 * CHUNKS, count)),
            pltpu.SemaphoreType.DMA((2 * CHUNKS, count)),
        ],
        compiler_params=pltpu.CompilerParams(
            collective_id=0, has_side_effects=True, vmem_limit_bytes=40 * 1024 * 1024
        ),
        name="panel",
    )(held_modes, snapshots)


def factor_kernel(gram_ref, panel_ref, basis_ref, factor_ref, schur, residual):
    size = gram_ref.shape[0]
    schur[...] = gram_ref[...]
    residual[...] = panel_ref[...]
    column = lax.broadcasted_iota(jnp.int32, (BLOCK, size), 1)

    def step(block, carry):
        start = pl.multiple_of(block * BLOCK, BLOCK)
        here = pl.ds(start, BLOCK)
        rows = [schur[pl.ds(pl.multiple_of(start + 8 * g, 8), 8), here] for g in range(BLOCK // 8)]
        upper, inverse = factor_block(rows)
        beyond = dot(inverse, schur[here, :], (1, 0))
        beyond = jnp.where(column >= start + BLOCK, beyond, 0.0)
        schur[...] -= dot(beyond, beyond, (0, 0))
        factor_ref[here, :] = beyond
        factor_ref[here, here] = upper
        part = dot(residual[:, here], inverse, (1, 1))
        basis_ref[:, here] = part
        residual[...] -= dot(part, beyond, (1, 0))
        return carry

    lax.fori_loop(0, size // BLOCK, step, 0)


def factor(gram, residual_panel):
    rows, size = residual_panel.shape
    return pl.pallas_call(
        factor_kernel,
        out_shape=(
            jax.ShapeDtypeStruct((rows, size), jnp.float32),
            jax.ShapeDtypeStruct((size, size), jnp.float32),
        ),
        in_specs=[pl.BlockSpec(memory_space=pltpu.VMEM)] * 2,
        out_specs=(pl.BlockSpec(memory_space=pltpu.VMEM),) * 2,
        scratch_shapes=[pltpu.VMEM((size, size), jnp.float32), pltpu.VMEM((rows, size), jnp.float32)],
        compiler_params=pltpu.CompilerParams(vmem_limit_bytes=32 * 1024 * 1024),
        name="factor",
    )(gram, residual_panel)


def local(held_modes, snapshots):
    cells, slab = lax.axis_size("cells"), lax.axis_size("slab")
    total_rows = held_modes.shape[0] * cells * slab
    size = snapshots.shape[1]
    line_count = cells // 2
    unit = 8 * 4 * line_count
    halves = (held_modes.shape[1] // 2, size // CHUNKS // 2)
    if slab == 4 and cells % 2 == 0 and size % (CHUNKS * BLOCK) == 0 and all(half % unit == 0 for half in halves):
        return factor(*panel(held_modes, snapshots, line_count, total_rows)[::-1])
    local_terms = lax.dot_general(
        held_modes, snapshots, (((0,), (0,)), ((), ())), preferred_element_type=jnp.float32
    )
    coefficients = lax.psum(local_terms, ("cells", "slab")) / total_rows
    residual_panel = snapshots.astype(jnp.float32) - jnp.dot(
        held_modes.astype(jnp.float32), coefficients, precision=HIGHEST
    )
    gram = lax.psum(dot(residual_panel, residual_panel, (0, 0)), ("cells", "slab")) / total_rows
    return factor(gram, residual_panel)


def solution(mesh):
    in_specs = (P(("cells", "slab"), None), P(("cells", "slab"), None))
    out_specs = (P(("cells", "slab"), None), P())
    return jax.shard_map(local, mesh=mesh, in_specs=in_specs, out_specs=out_specs, check_vma=False)
```

```python
import functools

import jax
import jax.numpy as jnp
from jax import lax
from jax.experimental import pallas as pl
from jax.experimental.pallas import tpu as pltpu
from jax.sharding import PartitionSpec as P

BLOCK = 128
MESH = pl.DeviceIdType.MESH
CHUNKS = 2
STEPS = 7
HIGHEST = lax.Precision.HIGHEST


def dot(first, second, dims):
    return lax.dot_general(
        first, second, ((dims[:1], dims[1:]), ((), ())), precision=HIGHEST, preferred_element_type=jnp.float32
    )


def factor_block(rows):
    groups = len(rows)
    lane = lax.broadcasted_iota(jnp.int32, (8, BLOCK), 1)
    sub = lax.broadcasted_iota(jnp.int32, (8, BLOCK), 0)
    rows = list(rows)
    upper, inverse = [], []

    def lanes(value, index):
        return jnp.broadcast_to(value[:, index : index + 1], (8, BLOCK))

    def subs(value, index):
        return jnp.broadcast_to(value[index : index + 1, :], (8, BLOCK))

    for group in range(groups):
        first = 8 * group
        panel = rows[group]
        columns = [lanes(panel, first + k) for k in range(8)]
        outer = [[lanes(rows[other], first + k) for k in range(8)] for other in range(group + 1, groups)]
        scaled = jnp.zeros((8, BLOCK), jnp.float32)
        diagonal = jnp.zeros((8, BLOCK), jnp.float32)
        for j in range(0, 8, 2):
            at_left, at_right = lane == first + j, lane == first + j + 1
            is_top, is_low = sub == j, sub == j + 1
            pair = is_top | is_low
            left, right = columns[j], columns[j + 1]
            a, b, c = subs(left, j), subs(right, j), subs(right, j + 1)
            root = lax.rsqrt(a * c - b * b)
            inverse_det = root * root
            root_a = lax.rsqrt(a)
            top, low = subs(panel, j), subs(panel, j + 1)
            low_factor = root_a * root
            low_raw = jnp.where(at_left, -b, a * low - b * top)
            scaled = jnp.where(is_top, top * root_a, jnp.where(is_low, low_raw * low_factor, scaled))
            diagonal = jnp.where(is_top, root_a, jnp.where(is_low, a * low_factor, diagonal))
            weight_top = jnp.where(pair, jnp.where(is_top, -1.0, 0.0), left)
            weight_low = jnp.where(pair, jnp.where(is_low, -1.0, 0.0), right)
            new_top = jnp.where(at_left, c, jnp.where(at_right, -b, c * top - b * low))
            new_low = jnp.where(at_left, -b, jnp.where(at_right, a, a * low - b * top))
            change = weight_top * new_top + weight_low * new_low
            panel = jnp.where(pair | at_left | at_right, 0.0, panel) - change * inverse_det
            for k in range(j + 2, 8):
                top, low = subs(columns[k], j), subs(columns[k], j + 1)
                change = weight_top * (c * top - b * low) + weight_low * (a * low - b * top)
                columns[k] = jnp.where(pair, 0.0, columns[k]) - change * inverse_det
        row_index = sub + first
        upper.append(jnp.where(lane >= row_index, scaled, 0.0))
        inverse.append(jnp.where(lane < row_index, scaled, jnp.where(lane == row_index, diagonal, 0.0)))
        solved = [subs(panel, k) for k in range(8)]
        kept = (lane < first) | (lane >= first + 8)
        for other in range(group + 1, groups):
            terms = [outer[other - group - 1][k] * solved[k] for k in range(8)]
            while len(terms) > 1:
                terms = [a + b for a, b in zip(terms[::2], terms[1::2])]
            rows[other] = jnp.where(kept, rows[other], 0.0) - terms[0]
    return jnp.concatenate(upper, 0), jnp.concatenate(inverse, 0)


class Part:
    def __init__(self, start, rows, stages):
        self.start, self.rows, self.stages, self.pending = start, rows, stages, []
        self.spans = [(start, rows)]
        for stage in stages:
            at, n = self.spans[-1]
            n //= stage["count"]
            self.spans.append((at + stage["index"] * n, n))


def slice_of(start, rows):
    return pl.ds(pl.multiple_of(start, 8), rows)


def all_reduce(acc, total, landing, places, produce, scale, send_sems, recv_sems, started):
    core, pair, plane, line = places
    half = acc.shape[0] // 2
    unit = 8 * plane["count"] * line["count"]
    long_rows = max(1, round(0.75 * (half // unit))) * unit
    used = [0]

    def copy(src, dst, device):
        index = used[0]
        used[0] += 1
        descriptor = pltpu.make_async_remote_copy(
            src_ref=src,
            dst_ref=dst,
            send_sem=send_sems.at[index],
            recv_sem=recv_sems.at[index],
            device_id=device,
            device_id_type=MESH,
        )
        descriptor.start()
        started.append(descriptor)
        return descriptor

    mine, other = core * half, (1 - core) * half
    bounds = [(0, long_rows, (plane, line))]
    if half > long_rows:
        bounds.append((long_rows, half - long_rows, (line, plane)))
    parts = [Part(mine + at, n, stages) for at, n, stages in bounds]
    slot = [0]

    def room(count, rows):
        at = slot[0]
        slot[0] += count * rows
        return [landing.at[pl.ds(at + k * rows, rows)] for k in range(count)]

    def send_scatter(part, level):
        stage = part.stages[level]
        at, _ = part.spans[level]
        n = part.spans[level + 1][1]
        spans = room(stage["count"] - 1, n)
        part.pending = [
            (copy(acc.at[slice_of(at + target * n, n)], span, device), span)
            for (target, device, _), span in zip(stage["peers"], spans)
        ]

    def finish_scatter(part, level):
        where = slice_of(*part.spans[level + 1])
        value = acc[where, :]
        for descriptor, span in part.pending:
            descriptor.wait_recv()
            value = value + span[...]
        if level + 1 == len(part.stages):
            total[where, :] = value * scale
        else:
            acc[where, :] = value

    def send_gather(part, level):
        where = slice_of(*part.spans[level + 1])
        part.pending = [
            copy(total.at[where], total.at[where], device) for _, device, _ in part.stages[level]["peers"]
        ]

    lasts = []

    def forward(start, n):
        where = slice_of(start, n)
        lasts.append(copy(total.at[where], total.at[where], pair))

    firsts = []
    for at, n, _ in bounds:
        produce(other + at, n)
        span = room(1, n)[0]
        firsts.append((copy(acc.at[slice_of(other + at, n)], span, pair), span))
    for at, n, _ in bounds:
        produce(mine + at, n)
    yield
    for part, (first, span) in zip(parts, firsts):
        first.wait_recv()
        where = slice_of(part.start, part.rows)
        acc[where, :] = acc[where, :] + span[...]
        send_scatter(part, 0)
    yield
    for level in (0, 1):
        for part in parts[::-1]:
            finish_scatter(part, level)
            if level == 0:
                send_scatter(part, 1)
            else:
                send_gather(part, 1)
        yield
    for part in parts[::-1]:
        for descriptor in part.pending:
            descriptor.wait_recv()
        send_gather(part, 0)
        forward(*part.spans[1])
    yield
    for part in parts[::-1]:
        at, _ = part.spans[0]
        n = part.spans[1][1]
        for descriptor, (_, _, source) in zip(part.pending, part.stages[0]["peers"]):
            descriptor.wait_recv()
            forward(at + source * n, n)
    yield
    for descriptor in lasts:
        descriptor.wait_recv()


def panel_kernel(
    line_count, total_rows, modes_hbm, snaps_hbm, residual_ref, gram_ref, modes_ref, snaps_ref, load_sems,
    terms, coefficients, landing, gram_terms, gram, gram_landing, send_sems, recv_sems,
):
    loads = [
        pltpu.make_async_copy(modes_hbm, modes_ref, load_sems.at[0]),
        pltpu.make_async_copy(snaps_hbm, snaps_ref, load_sems.at[1]),
    ]
    for load in loads:
        load.start()
    cells, slab = lax.axis_index("cells"), lax.axis_index("slab")
    z, x, y, core = cells // 2, cells % 2, slab // 2, slab % 2
    pair = {"cells": cells, "slab": y * 2 + (1 - core)}
    plane_peers = []
    for k in range(1, 4):
        there_x = 1 - x if k & 2 else x
        there_y = 1 - y if k & 1 else y
        device = {"cells": z * 2 + there_x, "slab": there_y * 2 + core}
        plane_peers.append((there_x * 2 + there_y, device, there_x * 2 + there_y))
    line_peers = []
    for k in range(1, line_count):
        ahead, behind = lax.rem(z + k, line_count), lax.rem(z + line_count - k, line_count)
        line_peers.append((ahead, {"cells": ahead * 2 + x, "slab": slab}, behind))
    plane = {"count": 4, "index": x * 2 + y, "peers": plane_peers}
    line = {"count": line_count, "index": z, "peers": line_peers}
    places = (core, pair, plane, line)

    devices = [pair] + [peer[1] for peer in plane_peers + line_peers]
    barrier = pltpu.get_barrier_semaphore()
    for device in devices:
        pl.semaphore_signal(barrier, inc=1, device_id=device, device_id_type=MESH)

    for load in loads:
        load.wait()

    started = []
    scale = 1.0 / total_rows
    entered = []
    size = residual_ref.shape[1]
    width = size // CHUNKS

    def coefficient_sum(chunk):
        acc = terms.at[chunk]

        def project(start, rows):
            wanted = modes_ref[:, pl.ds(pl.multiple_of(start, BLOCK), rows)]
            acc[slice_of(start, rows), :] = lax.dot_general(
                wanted, snaps_ref[:, chunk * width : (chunk + 1) * width], (((0,), (0,)), ((), ())),
                preferred_element_type=jnp.float32,
            )
            if not entered:
                pl.semaphore_wait(barrier, len(devices))
                entered.append(True)

        return all_reduce(
            acc, coefficients.at[chunk], landing.at[chunk], places, project, scale,
            send_sems.at[chunk], recv_sems.at[chunk], started,
        )

    def gram_sum(chunk):
        rows = pl.ds(0, (chunk + 1) * width)
        return all_reduce(
            gram_terms.at[chunk, rows], gram.at[chunk, rows], gram_landing.at[chunk], places, lambda start, n: None,
            scale, send_sems.at[CHUNKS + chunk], recv_sems.at[CHUNKS + chunk], started,
        )

    def times(part):
        return jnp.dot(modes_ref[...], part, preferred_element_type=jnp.float32)

    def subtract(chunk):
        columns = slice(chunk * width, (chunk + 1) * width)
        whole = coefficients[chunk]
        high = whole.astype(jnp.bfloat16)
        rest = whole - high.astype(jnp.float32)
        middle = rest.astype(jnp.bfloat16)
        low = (rest - middle.astype(jnp.float32)).astype(jnp.bfloat16)
        value = snaps_ref[:, columns].astype(jnp.float32) - (times(high) + (times(middle) + times(low)))
        residual_ref[:, columns] = value
        before = (chunk + 1) * width
        gram_terms[chunk, :before, :] = dot(residual_ref[:, :before], value, (0, 0))

    sums = [coefficient_sum(chunk) for chunk in range(CHUNKS)]
    gram_sums = [gram_sum(chunk) for chunk in range(CHUNKS)]
    for _ in range(STEPS - 1):
        for turn in sums:
            next(turn)
    for chunk in range(CHUNKS):
        next(sums[chunk], None)
        subtract(chunk)
        next(gram_sums[chunk])
    for _ in range(STEPS - 1):
        for turn in gram_sums:
            next(turn, None)
    for chunk in range(CHUNKS):
        before, columns = (chunk + 1) * width, slice(chunk * width, (chunk + 1) * width)
        gram_ref[:before, columns] = gram[chunk, :before, :]
        if before < size:
            gram_ref[before:, columns] = jnp.zeros((size - before, width), jnp.float32)
    for descriptor in started:
        descriptor.wait_send()


def panel(held_modes, snapshots, line_count, total_rows):
    rows, modes = held_modes.shape
    size = snapshots.shape[1]
    width = size // CHUNKS
    count = 2 * (1 + 2 * (3 + line_count - 1) + max(4, line_count))
    return pl.pallas_call(
        functools.partial(panel_kernel, line_count, total_rows),
        out_shape=(
            jax.ShapeDtypeStruct((rows, size), jnp.float32),
            jax.ShapeDtypeStruct((size, size), jnp.float32),
        ),
        in_specs=[pl.BlockSpec(memory_space=pltpu.HBM)] * 2,
        out_specs=(pl.BlockSpec(memory_space=pltpu.VMEM),) * 2,
        scratch_shapes=[
            pltpu.VMEM((rows, modes), held_modes.dtype),
            pltpu.VMEM((rows, size), snapshots.dtype),
            pltpu.SemaphoreType.DMA((2,)),
            pltpu.VMEM((CHUNKS, modes, width), jnp.float32),
            pltpu.VMEM((CHUNKS, modes, width), jnp.float32),
            pltpu.VMEM((CHUNKS, 2 * modes, width), jnp.float32),
            pltpu.VMEM((CHUNKS, size, width), jnp.float32),
            pltpu.VMEM((CHUNKS, size, width), jnp.float32),
            pltpu.VMEM((CHUNKS, 2 * size, width), jnp.float32),
            pltpu.SemaphoreType.DMA((2 * CHUNKS, count)),
            pltpu.SemaphoreType.DMA((2 * CHUNKS, count)),
        ],
        compiler_params=pltpu.CompilerParams(
            collective_id=0, has_side_effects=True, vmem_limit_bytes=40 * 1024 * 1024
        ),
        name="panel",
    )(held_modes, snapshots)


def factor_kernel(gram_ref, panel_ref, basis_ref, factor_ref, schur, residual):
    size = gram_ref.shape[0]
    schur[...] = gram_ref[...]
    residual[...] = panel_ref[...]
    index = lax.broadcasted_iota(jnp.int32, (BLOCK, BLOCK), 0)
    on_diagonal = index == lax.broadcasted_iota(jnp.int32, (BLOCK, BLOCK), 1)
    for start in range(0, size, BLOCK):
        end = start + BLOCK
        here = slice(start, end)
        block = schur[here, here]
        kept = jnp.where(on_diagonal, block, 0.0)
        along = jnp.sum(kept, axis=0, keepdims=True)
        scale = lax.rsqrt(along)
        block = block * scale * lax.rsqrt(jnp.sum(kept, axis=1, keepdims=True))
        upper, inverse = factor_block([block[8 * g : 8 * g + 8, :] for g in range(BLOCK // 8)])
        inverse = inverse * scale
        factor_ref[here, here] = upper * (along * scale)
        if start:
            factor_ref[here, :start] = jnp.zeros((BLOCK, start), jnp.float32)
        if end < size:
            beyond = dot(inverse, schur[here, end:], (1, 0))
            factor_ref[here, end:] = beyond
            for other in range(end, size, BLOCK):
                rows = slice(other, other + BLOCK)
                away = other - end
                schur[rows, other:] -= dot(beyond[:, away : away + BLOCK], beyond[:, away:], (0, 0))
        part = dot(residual[:, here], inverse, (1, 1))
        basis_ref[:, here] = part
        if end < size:
            residual[:, end:] -= dot(part, beyond, (1, 0))


def factor(gram, residual_panel):
    rows, size = residual_panel.shape
    return pl.pallas_call(
        factor_kernel,
        out_shape=(
            jax.ShapeDtypeStruct((rows, size), jnp.float32),
            jax.ShapeDtypeStruct((size, size), jnp.float32),
        ),
        in_specs=[pl.BlockSpec(memory_space=pltpu.VMEM)] * 2,
        out_specs=(pl.BlockSpec(memory_space=pltpu.VMEM),) * 2,
        scratch_shapes=[pltpu.VMEM((size, size), jnp.float32), pltpu.VMEM((rows, size), jnp.float32)],
        compiler_params=pltpu.CompilerParams(vmem_limit_bytes=32 * 1024 * 1024),
        name="factor",
    )(gram, residual_panel)


def local(held_modes, snapshots):
    cells, slab = lax.axis_size("cells"), lax.axis_size("slab")
    total_rows = held_modes.shape[0] * cells * slab
    size = snapshots.shape[1]
    line_count = cells // 2
    unit = 8 * 4 * line_count
    halves = (held_modes.shape[1] // 2, size // CHUNKS // 2)
    if slab == 4 and cells % 2 == 0 and size % (CHUNKS * BLOCK) == 0 and all(half % unit == 0 for half in halves):
        return factor(*panel(held_modes, snapshots, line_count, total_rows)[::-1])
    local_terms = lax.dot_general(
        held_modes, snapshots, (((0,), (0,)), ((), ())), preferred_element_type=jnp.float32
    )
    coefficients = lax.psum(local_terms, ("cells", "slab")) / total_rows
    residual_panel = snapshots.astype(jnp.float32) - jnp.dot(
        held_modes.astype(jnp.float32), coefficients, precision=HIGHEST
    )
    gram = lax.psum(dot(residual_panel, residual_panel, (0, 0)), ("cells", "slab")) / total_rows
    return factor(gram, residual_panel)


def solution(mesh):
    in_specs = (P(("cells", "slab"), None), P(("cells", "slab"), None))
    out_specs = (P(("cells", "slab"), None), P())
    return jax.shard_map(local, mesh=mesh, in_specs=in_specs, out_specs=out_specs, check_vma=False)
```

```python
import functools

import jax
import jax.numpy as jnp
from jax import lax
from jax.experimental import pallas as pl
from jax.experimental.pallas import tpu as pltpu
from jax.sharding import PartitionSpec as P

BLOCK = 128
MESH = pl.DeviceIdType.MESH
CHUNKS = 2
SPLIT = 2
STEPS = 7
HIGHEST = lax.Precision.HIGHEST


def dot(first, second, dims):
    return lax.dot_general(
        first, second, ((dims[:1], dims[1:]), ((), ())), precision=HIGHEST, preferred_element_type=jnp.float32
    )


def factor_block(rows):
    groups = len(rows)
    lane = lax.broadcasted_iota(jnp.int32, (8, BLOCK), 1)
    sub = lax.broadcasted_iota(jnp.int32, (8, BLOCK), 0)
    rows = list(rows)
    upper, inverse = [], []

    def lanes(value, index):
        return jnp.broadcast_to(value[:, index : index + 1], (8, BLOCK))

    def subs(value, index):
        return jnp.broadcast_to(value[index : index + 1, :], (8, BLOCK))

    for group in range(groups):
        first = 8 * group
        panel = rows[group]
        columns = [lanes(panel, first + k) for k in range(8)]
        outer = [[lanes(rows[other], first + k) for k in range(8)] for other in range(group + 1, groups)]
        scaled = jnp.zeros((8, BLOCK), jnp.float32)
        diagonal = jnp.zeros((8, BLOCK), jnp.float32)
        for j in range(0, 8, 2):
            at_left, at_right = lane == first + j, lane == first + j + 1
            is_top, is_low = sub == j, sub == j + 1
            pair = is_top | is_low
            left, right = columns[j], columns[j + 1]
            a, b, c = subs(left, j), subs(right, j), subs(right, j + 1)
            root = lax.rsqrt(a * c - b * b)
            inverse_det = root * root
            root_a = lax.rsqrt(a)
            top, low = subs(panel, j), subs(panel, j + 1)
            low_factor = root_a * root
            low_raw = jnp.where(at_left, -b, a * low - b * top)
            scaled = jnp.where(is_top, top * root_a, jnp.where(is_low, low_raw * low_factor, scaled))
            diagonal = jnp.where(is_top, root_a, jnp.where(is_low, a * low_factor, diagonal))
            weight_top = jnp.where(pair, jnp.where(is_top, -1.0, 0.0), left)
            weight_low = jnp.where(pair, jnp.where(is_low, -1.0, 0.0), right)
            new_top = jnp.where(at_left, c, jnp.where(at_right, -b, c * top - b * low))
            new_low = jnp.where(at_left, -b, jnp.where(at_right, a, a * low - b * top))
            change = weight_top * new_top + weight_low * new_low
            panel = jnp.where(pair | at_left | at_right, 0.0, panel) - change * inverse_det
            for k in range(j + 2, 8):
                top, low = subs(columns[k], j), subs(columns[k], j + 1)
                change = weight_top * (c * top - b * low) + weight_low * (a * low - b * top)
                columns[k] = jnp.where(pair, 0.0, columns[k]) - change * inverse_det
        row_index = sub + first
        upper.append(jnp.where(lane >= row_index, scaled, 0.0))
        inverse.append(jnp.where(lane < row_index, scaled, jnp.where(lane == row_index, diagonal, 0.0)))
        solved = [subs(panel, k) for k in range(8)]
        kept = (lane < first) | (lane >= first + 8)
        for other in range(group + 1, groups):
            terms = [outer[other - group - 1][k] * solved[k] for k in range(8)]
            while len(terms) > 1:
                terms = [a + b for a, b in zip(terms[::2], terms[1::2])]
            rows[other] = jnp.where(kept, rows[other], 0.0) - terms[0]
    return jnp.concatenate(upper, 0), jnp.concatenate(inverse, 0)


class Part:
    def __init__(self, start, rows, stages):
        self.start, self.rows, self.stages, self.pending = start, rows, stages, []
        self.spans = [(start, rows)]
        for stage in stages:
            at, n = self.spans[-1]
            n //= stage["count"]
            self.spans.append((at + stage["index"] * n, n))


def slice_of(start, rows):
    return pl.ds(pl.multiple_of(start, 8), rows)


def all_reduce(acc, total, landing, places, produce, scale, send_sems, recv_sems, started):
    core, pair, plane, line = places
    half = acc.shape[0] // 2
    unit = 8 * plane["count"] * line["count"]
    long_rows = max(1, round(0.75 * (half // unit))) * unit
    used = [0]

    def copy(src, dst, device):
        index = used[0]
        used[0] += 1
        descriptor = pltpu.make_async_remote_copy(
            src_ref=src,
            dst_ref=dst,
            send_sem=send_sems.at[index],
            recv_sem=recv_sems.at[index],
            device_id=device,
            device_id_type=MESH,
        )
        descriptor.start()
        started.append(descriptor)
        return descriptor

    mine, other = core * half, (1 - core) * half
    bounds = [(0, long_rows, (plane, line))]
    if half > long_rows:
        bounds.append((long_rows, half - long_rows, (line, plane)))
    parts = [Part(mine + at, n, stages) for at, n, stages in bounds]
    slot = [0]

    def room(count, rows):
        at = slot[0]
        slot[0] += count * rows
        return [landing.at[pl.ds(at + k * rows, rows)] for k in range(count)]

    def send_scatter(part, level):
        stage = part.stages[level]
        at, _ = part.spans[level]
        n = part.spans[level + 1][1]
        spans = room(stage["count"] - 1, n)
        part.pending = [
            (copy(acc.at[slice_of(at + target * n, n)], span, device), span)
            for (target, device, _), span in zip(stage["peers"], spans)
        ]

    def finish_scatter(part, level):
        where = slice_of(*part.spans[level + 1])
        value = acc[where, :]
        for descriptor, span in part.pending:
            descriptor.wait_recv()
            value = value + span[...]
        if level + 1 == len(part.stages):
            total[where, :] = value * scale
        else:
            acc[where, :] = value

    def send_gather(part, level):
        where = slice_of(*part.spans[level + 1])
        part.pending = [
            copy(total.at[where], total.at[where], device) for _, device, _ in part.stages[level]["peers"]
        ]

    lasts = []

    def forward(start, n):
        where = slice_of(start, n)
        lasts.append(copy(total.at[where], total.at[where], pair))

    firsts = []
    for at, n, _ in bounds:
        produce(other + at, n)
        span = room(1, n)[0]
        firsts.append((copy(acc.at[slice_of(other + at, n)], span, pair), span))
    for at, n, _ in bounds:
        produce(mine + at, n)
    yield
    for part, (first, span) in zip(parts, firsts):
        first.wait_recv()
        where = slice_of(part.start, part.rows)
        acc[where, :] = acc[where, :] + span[...]
        send_scatter(part, 0)
    yield
    for level in (0, 1):
        for part in parts[::-1]:
            finish_scatter(part, level)
            if level == 0:
                send_scatter(part, 1)
            else:
                send_gather(part, 1)
        yield
    for part in parts[::-1]:
        for descriptor in part.pending:
            descriptor.wait_recv()
        send_gather(part, 0)
        forward(*part.spans[1])
    yield
    for part in parts[::-1]:
        at, _ = part.spans[0]
        n = part.spans[1][1]
        for descriptor, (_, _, source) in zip(part.pending, part.stages[0]["peers"]):
            descriptor.wait_recv()
            forward(at + source * n, n)
    yield
    for descriptor in lasts:
        descriptor.wait_recv()


def panel_kernel(
    line_count, total_rows, modes_hbm, snaps_hbm, residual_ref, gram_ref, modes_ref, snaps_ref, load_sems,
    terms, coefficients, landing, gram_terms, gram, gram_landing, send_sems, recv_sems,
):
    loads = [
        pltpu.make_async_copy(modes_hbm, modes_ref, load_sems.at[0]),
        pltpu.make_async_copy(snaps_hbm, snaps_ref, load_sems.at[1]),
    ]
    for load in loads:
        load.start()
    cells, slab = lax.axis_index("cells"), lax.axis_index("slab")
    z, x, y, core = cells // 2, cells % 2, slab // 2, slab % 2
    pair = {"cells": cells, "slab": y * 2 + (1 - core)}
    plane_peers = []
    for k in range(1, 4):
        there_x = 1 - x if k & 2 else x
        there_y = 1 - y if k & 1 else y
        device = {"cells": z * 2 + there_x, "slab": there_y * 2 + core}
        plane_peers.append((there_x * 2 + there_y, device, there_x * 2 + there_y))
    line_peers = []
    for k in range(1, line_count):
        ahead, behind = lax.rem(z + k, line_count), lax.rem(z + line_count - k, line_count)
        line_peers.append((ahead, {"cells": ahead * 2 + x, "slab": slab}, behind))
    plane = {"count": 4, "index": x * 2 + y, "peers": plane_peers}
    line = {"count": line_count, "index": z, "peers": line_peers}
    places = (core, pair, plane, line)

    devices = [pair] + [peer[1] for peer in plane_peers + line_peers]
    barrier = pltpu.get_barrier_semaphore()
    for device in devices:
        pl.semaphore_signal(barrier, inc=1, device_id=device, device_id_type=MESH)

    for load in loads:
        load.wait()

    started = []
    scale = 1.0 / total_rows
    entered = []
    size = residual_ref.shape[1]
    width = size // CHUNKS
    narrow = width // SPLIT

    def coefficient_sum(chunk):
        acc = terms.at[chunk]

        def project(start, rows):
            wanted = modes_ref[:, pl.ds(pl.multiple_of(start, BLOCK), rows)]
            acc[slice_of(start, rows), :] = lax.dot_general(
                wanted, snaps_ref[:, chunk * narrow : (chunk + 1) * narrow], (((0,), (0,)), ((), ())),
                preferred_element_type=jnp.float32,
            )
            if not entered:
                pl.semaphore_wait(barrier, len(devices))
                entered.append(True)

        return all_reduce(
            acc, coefficients.at[chunk], landing.at[chunk], places, project, scale,
            send_sems.at[chunk], recv_sems.at[chunk], started,
        )

    def gram_sum(chunk):
        rows = pl.ds(0, (chunk + 1) * width)
        return all_reduce(
            gram_terms.at[chunk, rows], gram.at[chunk, rows], gram_landing.at[chunk], places, lambda start, n: None,
            scale, send_sems.at[SPLIT * CHUNKS + chunk], recv_sems.at[SPLIT * CHUNKS + chunk], started,
        )

    def times(part):
        return jnp.dot(modes_ref[...], part, preferred_element_type=jnp.float32)

    def subtract(chunk):
        columns = slice(chunk * width, (chunk + 1) * width)
        whole = jnp.concatenate([coefficients[SPLIT * chunk + k] for k in range(SPLIT)], axis=1)
        high = whole.astype(jnp.bfloat16)
        rest = whole - high.astype(jnp.float32)
        middle = rest.astype(jnp.bfloat16)
        low = (rest - middle.astype(jnp.float32)).astype(jnp.bfloat16)
        value = snaps_ref[:, columns].astype(jnp.float32) - (times(high) + (times(middle) + times(low)))
        residual_ref[:, columns] = value
        before = (chunk + 1) * width
        gram_terms[chunk, :before, :] = dot(residual_ref[:, :before], value, (0, 0))

    sums = [coefficient_sum(chunk) for chunk in range(SPLIT * CHUNKS)]
    gram_sums = [gram_sum(chunk) for chunk in range(CHUNKS)]
    for _ in range(STEPS - 1):
        for turn in sums:
            next(turn)
    for chunk in range(CHUNKS):
        for turn in sums[SPLIT * chunk : SPLIT * (chunk + 1)]:
            next(turn, None)
        subtract(chunk)
        next(gram_sums[chunk])
    for _ in range(STEPS - 1):
        for turn in gram_sums:
            next(turn, None)
    for chunk in range(CHUNKS):
        before, columns = (chunk + 1) * width, slice(chunk * width, (chunk + 1) * width)
        gram_ref[:before, columns] = gram[chunk, :before, :]
        if before < size:
            gram_ref[before:, columns] = jnp.zeros((size - before, width), jnp.float32)
    for descriptor in started:
        descriptor.wait_send()


def panel(held_modes, snapshots, line_count, total_rows):
    rows, modes = held_modes.shape
    size = snapshots.shape[1]
    width = size // CHUNKS
    count = 2 * (1 + 2 * (3 + line_count - 1) + max(4, line_count))
    return pl.pallas_call(
        functools.partial(panel_kernel, line_count, total_rows),
        out_shape=(
            jax.ShapeDtypeStruct((rows, size), jnp.float32),
            jax.ShapeDtypeStruct((size, size), jnp.float32),
        ),
        in_specs=[pl.BlockSpec(memory_space=pltpu.HBM)] * 2,
        out_specs=(pl.BlockSpec(memory_space=pltpu.VMEM),) * 2,
        scratch_shapes=[
            pltpu.VMEM((rows, modes), held_modes.dtype),
            pltpu.VMEM((rows, size), snapshots.dtype),
            pltpu.SemaphoreType.DMA((2,)),
            pltpu.VMEM((SPLIT * CHUNKS, modes, width // SPLIT), jnp.float32),
            pltpu.VMEM((SPLIT * CHUNKS, modes, width // SPLIT), jnp.float32),
            pltpu.VMEM((SPLIT * CHUNKS, 2 * modes, width // SPLIT), jnp.float32),
            pltpu.VMEM((CHUNKS, size, width), jnp.float32),
            pltpu.VMEM((CHUNKS, size, width), jnp.float32),
            pltpu.VMEM((CHUNKS, 2 * size, width), jnp.float32),
            pltpu.SemaphoreType.DMA(((SPLIT + 1) * CHUNKS, count)),
            pltpu.SemaphoreType.DMA(((SPLIT + 1) * CHUNKS, count)),
        ],
        compiler_params=pltpu.CompilerParams(
            collective_id=0, has_side_effects=True, vmem_limit_bytes=40 * 1024 * 1024
        ),
        name="panel",
    )(held_modes, snapshots)


def factor_kernel(gram_ref, panel_ref, basis_ref, factor_ref, schur, residual):
    size = gram_ref.shape[0]
    schur[...] = gram_ref[...]
    residual[...] = panel_ref[...]
    index = lax.broadcasted_iota(jnp.int32, (BLOCK, BLOCK), 0)
    on_diagonal = index == lax.broadcasted_iota(jnp.int32, (BLOCK, BLOCK), 1)
    for start in range(0, size, BLOCK):
        end = start + BLOCK
        here = slice(start, end)
        block = schur[here, here]
        kept = jnp.where(on_diagonal, block, 0.0)
        along = jnp.sum(kept, axis=0, keepdims=True)
        scale = lax.rsqrt(along)
        block = block * scale * lax.rsqrt(jnp.sum(kept, axis=1, keepdims=True))
        upper, inverse = factor_block([block[8 * g : 8 * g + 8, :] for g in range(BLOCK // 8)])
        inverse = inverse * scale
        factor_ref[here, here] = upper * (along * scale)
        if start:
            factor_ref[here, :start] = jnp.zeros((BLOCK, start), jnp.float32)
        if end < size:
            beyond = dot(inverse, schur[here, end:], (1, 0))
            factor_ref[here, end:] = beyond
            for other in range(end, size, BLOCK):
                rows = slice(other, other + BLOCK)
                away = other - end
                schur[rows, other:] -= dot(beyond[:, away : away + BLOCK], beyond[:, away:], (0, 0))
        part = dot(residual[:, here], inverse, (1, 1))
        basis_ref[:, here] = part
        if end < size:
            residual[:, end:] -= dot(part, beyond, (1, 0))


def factor(gram, residual_panel):
    rows, size = residual_panel.shape
    return pl.pallas_call(
        factor_kernel,
        out_shape=(
            jax.ShapeDtypeStruct((rows, size), jnp.float32),
            jax.ShapeDtypeStruct((size, size), jnp.float32),
        ),
        in_specs=[pl.BlockSpec(memory_space=pltpu.VMEM)] * 2,
        out_specs=(pl.BlockSpec(memory_space=pltpu.VMEM),) * 2,
        scratch_shapes=[pltpu.VMEM((size, size), jnp.float32), pltpu.VMEM((rows, size), jnp.float32)],
        compiler_params=pltpu.CompilerParams(vmem_limit_bytes=32 * 1024 * 1024),
        name="factor",
    )(gram, residual_panel)


def local(held_modes, snapshots):
    cells, slab = lax.axis_size("cells"), lax.axis_size("slab")
    total_rows = held_modes.shape[0] * cells * slab
    size = snapshots.shape[1]
    line_count = cells // 2
    unit = 8 * 4 * line_count
    halves = (held_modes.shape[1] // 2, size // CHUNKS // 2)
    if slab == 4 and cells % 2 == 0 and size % (SPLIT * CHUNKS * BLOCK) == 0 and all(half % unit == 0 for half in halves):
        return factor(*panel(held_modes, snapshots, line_count, total_rows)[::-1])
    local_terms = lax.dot_general(
        held_modes, snapshots, (((0,), (0,)), ((), ())), preferred_element_type=jnp.float32
    )
    coefficients = lax.psum(local_terms, ("cells", "slab")) / total_rows
    residual_panel = snapshots.astype(jnp.float32) - jnp.dot(
        held_modes.astype(jnp.float32), coefficients, precision=HIGHEST
    )
    gram = lax.psum(dot(residual_panel, residual_panel, (0, 0)), ("cells", "slab")) / total_rows
    return factor(gram, residual_panel)


def solution(mesh):
    in_specs = (P(("cells", "slab"), None), P(("cells", "slab"), None))
    out_specs = (P(("cells", "slab"), None), P())
    return jax.shard_map(local, mesh=mesh, in_specs=in_specs, out_specs=out_specs, check_vma=False)
```
